32 devices in a mesh: dp: 4 (over z), expert: 8 (over y, x, core).
Axes of the slice: x: 2, y: 2, z: 4, core: 2. Of those that a mesh axis runs over, the one named last changes fastest.
Arguments:
- tokens: bfloat16 [4096, 4096], P(('dp', 'expert')), may hold values from -6 to 6
- cotangent: bfloat16 [4096, 4096], P(('dp', 'expert')), may hold values from -0.796875 to 0.796875
- router_probs: float32 [4096, 4], P(('dp', 'expert')), may hold values from 0.1 to 1
- routing: int32 [4096, 4], P(('dp', 'expert')), may hold values from 0 to 31, all different within a row
- hot_marks: int32 [32], replicated, may hold values from 0 to 1, as said below
- cap_counts: int32 [32], replicated, may hold values from 8 to 16, as said below
- gate_up: bfloat16 [32, 2, 4096, 768], P(('dp', 'expert')), may hold values from -0.09375 to 0.09375
- adapter_in: bfloat16 [32, 32, 768], P(('dp', 'expert')), may hold values from -0.21875 to 0.21875
- adapter_out: bfloat16 [32, 32, 4096], P(('dp', 'expert')), may hold values from -0.09375 to 0.09375
Outputs:
- in_gradient: float32 [32, 32, 768], P(('dp', 'expert'))
- out_gradient: float32 [32, 32, 4096], P(('dp', 'expert'))
The draws below stay inside these ranges and needn't reach their ends.
Inputs may be any that keep to these rules, and one draw needn't show every extreme that they name: `routing`: each token names 4 different experts. `hot_marks`: of every two experts whose numbers differ only in the bit of value 8 / 2, exactly one is marked. `cap_counts`: some expert's count equals 16.
All inputs are finite; a program needn't handle non-finite values.
Results may differ from the reference program's by a relative error of at most 0.005.
Values may be sent and summed in bfloat16 or wider, within the bound.
A program may use at most 192 MiB of HBM per device.

```python
import jax
import jax.numpy as jnp
from jax import lax

D = 4096
FF = 768
RANK = 32
TOPK = 4
TOK_DEV = 128
EXPERTS = 32
TOKENS = 4096
CAP = 16
N_EXPERT = 8
DEVICES = 32


def draw_hot_marks(key, part):
    expert_ids = jnp.arange(EXPERTS, dtype=jnp.int32)
    coins = jax.random.randint(key, (EXPERTS,), 0, 2).astype(jnp.int32)
    partner = jnp.bitwise_xor(expert_ids, N_EXPERT // 2)
    lower_half = expert_ids % N_EXPERT < N_EXPERT // 2
    return jnp.where(lower_half, coins, 1 - coins[partner]).astype(jnp.int32)


def draw_cap_counts(key, part):
    lowest = (CAP + 1) // 2
    values = jax.random.randint(key, (EXPERTS,), lowest, CAP + 1).astype(jnp.int32)
    filled = jax.random.randint(jax.random.fold_in(key, 7), (EXPERTS,), 0, 4) == 0
    values = jnp.where(filled, CAP, values)
    chosen = jax.random.randint(jax.random.fold_in(key, 11), (), 0, EXPERTS)
    return values.at[chosen].set(CAP).astype(jnp.int32)


def steps_of(stream_key, shape, cuts, smallest, high):
    level, own = 1.0, jax.random.fold_in(stream_key, 6)
    for position, blocks in cuts:
        heights = jnp.exp(jax.random.uniform(jax.random.fold_in(own, position), (blocks,), jnp.float32, smallest / len(cuts), high / len(cuts)))
        level = level * jnp.repeat(heights, shape[position] // blocks).reshape([-1 if axis == position else 1 for axis in range(len(shape))])
    return level


def different_ones(stream_key, rows, count, top, lift):
    order = jax.random.permutation(jax.random.fold_in(stream_key, 1), count)
    pull = order
    for power in range(3):
        pull = pull * pull // count
    pull = pull * lift // count
    lots = jax.random.randint(jax.random.fold_in(stream_key, 2), (rows, count), 0, 4096) + pull
    sure = jax.random.permutation(jax.random.fold_in(stream_key, 3), rows)[jnp.arange(count) % rows]
    lots = jnp.where(jnp.arange(rows)[:, None] == sure[None, :], 1 << 14, lots)
    priority = lots * count + jnp.arange(count)
    return lax.top_k(priority.astype(jnp.int32), top)[1].astype(jnp.int32)


def gaussian(rng, shape, width, reach, split=(), kind=jnp.bfloat16):
    entries = jax.random.normal(rng, shape, jnp.float32) * width
    if len(split) > 0:
        entries = steps_of(rng, shape, split, -0.22, 0.18) * entries
    return jnp.clip(entries, min=-reach, max=reach).astype(kind)


def setup_inputs(seed: int = 0) -> dict:
    streams_of = jax.random.split(jax.random.key(seed), 10)
    return {
        "tokens": gaussian(streams_of[0], (TOKENS, D), 1.0, 6.0, ((0, 32),)),
        "cotangent": gaussian(streams_of[1], (TOKENS, D), 0.1, 0.796875, ((0, 32),)),
        "router_probs": jnp.clip(0.1 + 0.9 * jax.random.uniform(streams_of[2], (TOKENS, TOPK), jnp.float32) ** steps_of(streams_of[2], (TOKENS, TOPK), ((0, 32),), -0.2, 0.2), 0.1, 1.0),
        "routing": different_ones(streams_of[3], TOKENS, EXPERTS, TOPK, 2048),
        "hot_marks": draw_hot_marks(jax.random.fold_in(streams_of[9], 71), 0),
        "cap_counts": draw_cap_counts(jax.random.fold_in(streams_of[9], 71), 0),
        "gate_up": gaussian(streams_of[6], (EXPERTS, 2, D, FF), D ** -0.5, 0.09375, ((0, 32),)),
        "adapter_in": gaussian(streams_of[7], (EXPERTS, RANK, FF), FF ** -0.5, 0.21875, ((0, 32),)),
        "adapter_out": gaussian(streams_of[8], (EXPERTS, RANK, D), D ** -0.5, 0.09375, ((0, 32),)),
    }


adapter_scale_factor = 2.0


def reference(tokens, cotangent, router_probs, routing, hot_marks, cap_counts, gate_up, adapter_in, adapter_out):
    pair_count = TOK_DEV * TOPK
    flat_route = routing.reshape(DEVICES, pair_count)
    expert_ids = jnp.arange(EXPERTS, dtype=jnp.int32)

    def rank_block(route_row):
        onehot = (route_row[:, None] == expert_ids[None, :]).astype(jnp.int32)
        return jnp.sum((jnp.cumsum(onehot, axis=0) - onehot) * onehot, axis=1)

    order_rank = lax.map(rank_block, flat_route)
    limit_rows = cap_counts + CAP * hot_marks
    kept_mask = order_rank < limit_rows[flat_route]
    slot_width = 2 * CAP
    source = jnp.broadcast_to(jnp.arange(DEVICES, dtype=jnp.int32)[:, None], flat_route.shape)
    pair_ids = jnp.arange(DEVICES * pair_count, dtype=jnp.int32).reshape(DEVICES, pair_count)
    column = jnp.where(kept_mask, order_rank, slot_width).astype(jnp.int32)
    slot_table = jnp.full((DEVICES, EXPERTS, slot_width + 1), -1, jnp.int32)
    slot_table = slot_table.at[source, flat_route, column].set(pair_ids)[:, :, :slot_width]
    probs_flat = router_probs.reshape(-1)

    def one_expert(expert):
        chosen = lax.dynamic_index_in_dim(slot_table, expert, 1, keepdims=False).reshape(-1)
        valid_rows = chosen >= 0
        safe_ids = jnp.maximum(chosen, 0)
        token_ids = safe_ids // TOPK
        inputs = tokens[token_ids]
        factor = jnp.where(valid_rows, probs_flat[safe_ids], 0.0)
        scaled_adapter_output = (factor[:, None] * cotangent[token_ids].astype(jnp.float32)).astype(jnp.bfloat16)
        weights = lax.dynamic_index_in_dim(gate_up, expert, 0, keepdims=False)
        gate_out = jnp.dot(inputs, weights[0], preferred_element_type=jnp.float32)
        up_out = jnp.dot(inputs, weights[1], preferred_element_type=jnp.float32)
        hidden_state_rows = (jax.nn.silu(gate_out) * up_out).astype(jnp.bfloat16)
        adapter_down_matrix = lax.dynamic_index_in_dim(adapter_in, expert, 0, keepdims=False)
        adapter_up_matrix = lax.dynamic_index_in_dim(adapter_out, expert, 0, keepdims=False)
        rank_projected_rows = (adapter_scale_factor * jnp.dot(hidden_state_rows, adapter_down_matrix.T, preferred_element_type=jnp.float32)).astype(jnp.bfloat16)
        rank_gradient_rows = (adapter_scale_factor * jnp.dot(scaled_adapter_output, adapter_up_matrix.T, preferred_element_type=jnp.float32)).astype(jnp.bfloat16)
        grad_first = jnp.dot(rank_gradient_rows.T, hidden_state_rows, preferred_element_type=jnp.float32)
        grad_second = jnp.dot(rank_projected_rows.T, scaled_adapter_output, preferred_element_type=jnp.float32)
        return grad_first, grad_second

    in_gradient, out_gradient = lax.map(one_expert, expert_ids)
    return in_gradient, out_gradient
```

```python
import jax
import jax.numpy as jnp
from jax import lax
from jax.sharding import PartitionSpec as P

adapter_scale_factor = 2.0


def hidden_units(inputs, weights):
    gate_out = jnp.dot(inputs, weights[0], preferred_element_type=jnp.float32)
    up_out = jnp.dot(inputs, weights[1], preferred_element_type=jnp.float32)
    return (jax.nn.silu(gate_out) * up_out).astype(jnp.bfloat16)


def body(
    tokens,
    cotangent,
    router_probs,
    routing,
    hot_marks,
    cap_counts,
    gate_up,
    adapter_in,
    adapter_out,
):
    tok_count, model_width = tokens.shape
    top_count = routing.shape[1]
    expert_total = cap_counts.shape[0]
    capacity = tok_count * top_count // expert_total
    per_dest = 2 * capacity
    dp_count = lax.axis_size("dp")
    group = lax.axis_size("expert")

    routed = jnp.concatenate([routing.astype(jnp.float32), router_probs], axis=1)
    routed = lax.all_gather(routed, "dp", axis=0, tiled=False)
    all_tokens = lax.all_gather(tokens, "dp", axis=0, tiled=False)
    all_cotangent = lax.all_gather(cotangent, "dp", axis=0, tiled=False)

    first_expert = lax.axis_index("dp") * group
    own_experts = first_expert + jnp.arange(group, dtype=jnp.int32)
    limits = cap_counts + capacity * hot_marks
    own_limits = lax.dynamic_slice_in_dim(limits, first_expert, group).astype(jnp.float32)
    routes = routed[:, :, :top_count]
    probs = routed[:, :, top_count:]
    named = routes[:, None, :, :] == own_experts.astype(jnp.float32)[None, :, None, None]
    member = jnp.any(named, axis=3)
    weight = jnp.sum(jnp.where(named, probs[:, None, :, :], 0.0), axis=3)
    at = jnp.arange(tok_count, dtype=jnp.int32)
    earlier = (at[:, None] < at[None, :]).astype(jnp.bfloat16)
    rank = jnp.einsum(
        "bet,tu->beu", member.astype(jnp.bfloat16), earlier, preferred_element_type=jnp.float32
    )
    kept = member & (rank < own_limits[None, :, None])
    column = jnp.where(kept, rank, -1.0).astype(jnp.int32)
    slots = jnp.arange(per_dest, dtype=jnp.int32)
    chosen = column[:, :, None, :] == slots[None, None, :, None]
    factor = jnp.sum(jnp.where(chosen, weight[:, :, None, :], 0.0), axis=3)
    chosen = chosen.astype(jnp.bfloat16).reshape(dp_count, group * per_dest, tok_count)
    factor = factor.reshape(dp_count, group * per_dest)

    def exchange(rows):
        rows = rows.reshape(dp_count, group, per_dest, model_width).swapaxes(0, 1)
        rows = lax.all_to_all(rows, "expert", split_axis=0, concat_axis=0, tiled=True)
        return rows.reshape(dp_count * group * per_dest, model_width)

    token_rows = jnp.einsum(
        "bst,btd->bsd", chosen, all_tokens, preferred_element_type=jnp.float32
    ).astype(jnp.bfloat16)
    inputs = exchange(token_rows)
    cotangent_rows = jnp.einsum(
        "bst,btd->bsd", chosen, all_cotangent, preferred_element_type=jnp.float32
    )
    scaled = exchange((factor[:, :, None] * cotangent_rows).astype(jnp.bfloat16))

    hidden = hidden_units(inputs, gate_up[0])
    low = (
        adapter_scale_factor
        * jnp.einsum("pn,cn->pc", hidden, adapter_in[0], preferred_element_type=jnp.float32)
    ).astype(jnp.bfloat16)
    back = (
        adapter_scale_factor
        * jnp.einsum("vw,cw->vc", scaled, adapter_out[0], preferred_element_type=jnp.float32)
    ).astype(jnp.bfloat16)
    grad_first = jnp.einsum("mr,mf->rf", back, hidden, preferred_element_type=jnp.float32)
    grad_second = jnp.einsum("mr,md->rd", low, scaled, preferred_element_type=jnp.float32)
    return (grad_first[None], grad_second[None])


def solution(mesh):
    in_specs = (
        P(("dp", "expert"), None),
        P(("dp", "expert"), None),
        P(("dp", "expert"), None),
        P(("dp", "expert"), None),
        P(),
        P(),
        P(("dp", "expert"), None, None, None),
        P(("dp", "expert"), None, None),
        P(("dp", "expert"), None, None),
    )
    out_specs = (P(("dp", "expert"), None, None), P(("dp", "expert"), None, None))
    return jax.shard_map(body, mesh=mesh, in_specs=in_specs, out_specs=out_specs, check_vma=False)
```

```python
import functools

import jax
import jax.numpy as jnp
from jax import lax
from jax.experimental import pallas as pl
from jax.experimental.pallas import tpu as pltpu
from jax.sharding import PartitionSpec as P

adapter_scale_factor = 2.0


PIECES = 2


def pick_kernel(scale, chosen_ref, factor_ref, rows_ref, out_ref):
    picked = jnp.dot(chosen_ref[0], rows_ref[0], preferred_element_type=jnp.float32)
    if scale:
        picked = factor_ref[0] * picked
    out_ref[...] = picked.reshape(out_ref.shape).astype(out_ref.dtype)


def pick(chosen, factor, rows, group, scale):
    blocks, tok_count, width = rows.shape
    picked_count = chosen.shape[1]
    per_dest = picked_count // group
    tile = min(width, 1024)
    return pl.pallas_call(
        functools.partial(pick_kernel, scale),
        grid=(blocks, width // tile),
        in_specs=[
            pl.BlockSpec((1, picked_count, tok_count), lambda b, j: (b, 0, 0)),
            pl.BlockSpec((1, picked_count, 1), lambda b, j: (b, 0, 0)),
            pl.BlockSpec((1, tok_count, tile), lambda b, j: (b, 0, j)),
        ],
        out_specs=pl.BlockSpec((group, 1, per_dest, tile), lambda b, j: (0, b, 0, j)),
        out_shape=jax.ShapeDtypeStruct((group, blocks, per_dest, width), rows.dtype),
        compiler_params=pltpu.CompilerParams(vmem_limit_bytes=56 * 1024 * 1024),
        cost_estimate=pl.CostEstimate(
            flops=2 * blocks * picked_count * tok_count * width,
            bytes_accessed=2 * blocks * (tok_count + picked_count) * width,
            transcendentals=0,
        ),
    )(chosen, factor, rows)


def body(
    tokens,
    cotangent,
    router_probs,
    routing,
    hot_marks,
    cap_counts,
    gate_up,
    adapter_in,
    adapter_out,
):
    tok_count, model_width = tokens.shape
    top_count = routing.shape[1]
    expert_total = cap_counts.shape[0]
    capacity = tok_count * top_count // expert_total
    per_dest = 2 * capacity
    dp_count = lax.axis_size("dp")
    group = lax.axis_size("expert")

    routed = jnp.concatenate([routing.astype(jnp.float32), router_probs], axis=1)
    routed = lax.all_gather(routed, "dp", axis=0, tiled=False)
    piece = model_width // PIECES
    spans = [slice(p * piece, (p + 1) * piece) for p in range(PIECES)]
    gathered = []
    for source in (tokens, cotangent):
        for span in spans:
            part = source[:, span]
            if gathered:
                part, gathered[-1] = lax.optimization_barrier((part, gathered[-1]))
            gathered.append(lax.all_gather(part, "dp", axis=0, tiled=False))

    first_expert = lax.axis_index("dp") * group
    own_experts = first_expert + jnp.arange(group, dtype=jnp.int32)
    limits = cap_counts + capacity * hot_marks
    own_limits = lax.dynamic_slice_in_dim(limits, first_expert, group).astype(jnp.float32)
    routes = routed[:, :, :top_count]
    probs = routed[:, :, top_count:]
    named = routes[:, None, :, :] == own_experts.astype(jnp.float32)[None, :, None, None]
    member = jnp.any(named, axis=3)
    weight = jnp.sum(jnp.where(named, probs[:, None, :, :], 0.0), axis=3)
    at = jnp.arange(tok_count, dtype=jnp.int32)
    earlier = (at[:, None] < at[None, :]).astype(jnp.bfloat16)
    rank = jnp.einsum(
        "bet,tu->beu", member.astype(jnp.bfloat16), earlier, preferred_element_type=jnp.float32
    )
    kept = member & (rank < own_limits[None, :, None])
    column = jnp.where(kept, rank, -1.0).astype(jnp.int32)
    slots = jnp.arange(per_dest, dtype=jnp.int32)
    chosen = column[:, :, None, :] == slots[None, None, :, None]
    factor = jnp.sum(jnp.where(chosen, weight[:, :, None, :], 0.0), axis=3)
    chosen = chosen.astype(jnp.bfloat16).reshape(dp_count, group * per_dest, tok_count)
    factor = factor.reshape(dp_count, group * per_dest, 1)

    def exchange(rows):
        rows = lax.all_to_all(rows, "expert", split_axis=0, concat_axis=0, tiled=True)
        return rows.reshape(dp_count * group * per_dest, piece)

    arrived = []
    for place, rows in enumerate(gathered):
        arrived.append(exchange(pick(chosen, factor, rows, group, place >= PIECES)))
    inputs, scaled = arrived[:PIECES], arrived[PIECES:]

    gate_out = sum(
        jnp.dot(x, gate_up[0, 0, span], preferred_element_type=jnp.float32)
        for x, span in zip(inputs, spans)
    )
    up_out = sum(
        jnp.dot(x, gate_up[0, 1, span], preferred_element_type=jnp.float32)
        for x, span in zip(inputs, spans)
    )
    hidden = (jax.nn.silu(gate_out) * up_out).astype(jnp.bfloat16)
    low = (
        adapter_scale_factor
        * jnp.einsum("pn,cn->pc", hidden, adapter_in[0], preferred_element_type=jnp.float32)
    ).astype(jnp.bfloat16)
    back = sum(
        jnp.einsum("vw,cw->vc", x, adapter_out[0, :, span], preferred_element_type=jnp.float32)
        for x, span in zip(scaled, spans)
    )
    back = (adapter_scale_factor * back).astype(jnp.bfloat16)
    grad_first = jnp.einsum("mr,mf->rf", back, hidden, preferred_element_type=jnp.float32)
    grad_second = jnp.concatenate(
        [jnp.einsum("mr,md->rd", low, x, preferred_element_type=jnp.float32) for x in scaled],
        axis=1,
    )
    return (grad_first[None], grad_second[None])


def solution(mesh):
    in_specs = (
        P(("dp", "expert"), None),
        P(("dp", "expert"), None),
        P(("dp", "expert"), None),
        P(("dp", "expert"), None),
        P(),
        P(),
        P(("dp", "expert"), None, None, None),
        P(("dp", "expert"), None, None),
        P(("dp", "expert"), None, None),
    )
    out_specs = (P(("dp", "expert"), None, None), P(("dp", "expert"), None, None))
    return jax.shard_map(body, mesh=mesh, in_specs=in_specs, out_specs=out_specs, check_vma=False)
```

```python
import functools

import jax
import jax.numpy as jnp
from jax import lax
from jax.experimental import pallas as pl
from jax.experimental.pallas import tpu as pltpu
from jax.sharding import PartitionSpec as P

adapter_scale_factor = 2.0


PIECES = 2


def pick_kernel(scale, chosen_ref, factor_ref, rows_ref, out_ref):
    picked = jnp.dot(chosen_ref[0], rows_ref[0], preferred_element_type=jnp.float32)
    if scale:
        picked = factor_ref[0] * picked
    out_ref[...] = picked.reshape(out_ref.shape).astype(out_ref.dtype)


def pick(chosen, factor, rows, group, scale):
    blocks, tok_count, width = rows.shape
    picked_count = chosen.shape[1]
    per_dest = picked_count // group
    tile = min(width, 1024)
    return pl.pallas_call(
        functools.partial(pick_kernel, scale),
        grid=(blocks, width // tile),
        in_specs=[
            pl.BlockSpec((1, picked_count, tok_count), lambda b, j: (b, 0, 0)),
            pl.BlockSpec((1, picked_count, 1), lambda b, j: (b, 0, 0)),
            pl.BlockSpec((1, tok_count, tile), lambda b, j: (b, 0, j)),
        ],
        out_specs=pl.BlockSpec((group, 1, per_dest, tile), lambda b, j: (0, b, 0, j)),
        out_shape=jax.ShapeDtypeStruct((group, blocks, per_dest, width), rows.dtype),
        compiler_params=pltpu.CompilerParams(vmem_limit_bytes=56 * 1024 * 1024),
        cost_estimate=pl.CostEstimate(
            flops=64 * blocks * picked_count * tok_count * width,
            bytes_accessed=64 * blocks * (tok_count + picked_count) * width,
            transcendentals=0,
        ),
    )(chosen, factor, rows)


def body(
    tokens,
    cotangent,
    router_probs,
    routing,
    hot_marks,
    cap_counts,
    gate_up,
    adapter_in,
    adapter_out,
):
    tok_count, model_width = tokens.shape
    top_count = routing.shape[1]
    expert_total = cap_counts.shape[0]
    capacity = tok_count * top_count // expert_total
    per_dest = 2 * capacity
    dp_count = lax.axis_size("dp")
    group = lax.axis_size("expert")

    routed = jnp.concatenate([routing.astype(jnp.float32), router_probs], axis=1)
    routed = lax.all_gather(routed, "dp", axis=0, tiled=False)
    piece = model_width // PIECES
    spans = [slice(p * piece, (p + 1) * piece) for p in range(PIECES)]
    gathered = []
    for source in (tokens, cotangent):
        for span in spans:
            part = source[:, span]
            if gathered:
                part, gathered[-1] = lax.optimization_barrier((part, gathered[-1]))
            gathered.append(lax.all_gather(part, "dp", axis=0, tiled=False))

    first_expert = lax.axis_index("dp") * group
    own_experts = first_expert + jnp.arange(group, dtype=jnp.int32)
    limits = cap_counts + capacity * hot_marks
    own_limits = lax.dynamic_slice_in_dim(limits, first_expert, group).astype(jnp.float32)
    routes = routed[:, :, :top_count]
    probs = routed[:, :, top_count:]
    named = routes[:, None, :, :] == own_experts.astype(jnp.float32)[None, :, None, None]
    member = jnp.any(named, axis=3)
    weight = jnp.sum(jnp.where(named, probs[:, None, :, :], 0.0), axis=3)
    at = jnp.arange(tok_count, dtype=jnp.int32)
    earlier = (at[:, None] < at[None, :]).astype(jnp.bfloat16)
    rank = jnp.einsum(
        "bet,tu->beu", member.astype(jnp.bfloat16), earlier, preferred_element_type=jnp.float32
    )
    kept = member & (rank < own_limits[None, :, None])
    column = jnp.where(kept, rank, -1.0).astype(jnp.int32)
    slots = jnp.arange(per_dest, dtype=jnp.int32)
    chosen = column[:, :, None, :] == slots[None, None, :, None]
    factor = jnp.sum(jnp.where(chosen, weight[:, :, None, :], 0.0), axis=3)
    chosen = chosen.astype(jnp.bfloat16).reshape(dp_count, group * per_dest, tok_count)
    factor = factor.reshape(dp_count, group * per_dest, 1)

    def exchange(rows):
        rows = lax.all_to_all(rows, "expert", split_axis=0, concat_axis=0, tiled=True)
        return rows.reshape(dp_count * group * per_dest, piece)

    arrived = []
    for place, rows in enumerate(gathered):
        arrived.append(exchange(pick(chosen, factor, rows, group, place >= PIECES)))
    inputs, scaled = arrived[:PIECES], arrived[PIECES:]

    gate_out = sum(
        jnp.dot(x, gate_up[0, 0, span], preferred_element_type=jnp.float32)
        for x, span in zip(inputs, spans)
    )
    up_out = sum(
        jnp.dot(x, gate_up[0, 1, span], preferred_element_type=jnp.float32)
        for x, span in zip(inputs, spans)
    )
    hidden = (jax.nn.silu(gate_out) * up_out).astype(jnp.bfloat16)
    low = (
        adapter_scale_factor
        * jnp.einsum("pn,cn->pc", hidden, adapter_in[0], preferred_element_type=jnp.float32)
    ).astype(jnp.bfloat16)
    back = sum(
        jnp.einsum("vw,cw->vc", x, adapter_out[0, :, span], preferred_element_type=jnp.float32)
        for x, span in zip(scaled, spans)
    )
    back = (adapter_scale_factor * back).astype(jnp.bfloat16)
    grad_first = jnp.einsum("mr,mf->rf", back, hidden, preferred_element_type=jnp.float32)
    grad_second = jnp.concatenate(
        [jnp.einsum("mr,md->rd", low, x, preferred_element_type=jnp.float32) for x in scaled],
        axis=1,
    )
    return (grad_first[None], grad_second[None])


def solution(mesh):
    in_specs = (
        P(("dp", "expert"), None),
        P(("dp", "expert"), None),
        P(("dp", "expert"), None),
        P(("dp", "expert"), None),
        P(),
        P(),
        P(("dp", "expert"), None, None, None),
        P(("dp", "expert"), None, None),
        P(("dp", "expert"), None, None),
    )
    out_specs = (P(("dp", "expert"), None, None), P(("dp", "expert"), None, None))
    return jax.shard_map(body, mesh=mesh, in_specs=in_specs, out_specs=out_specs, check_vma=False)
```
